256 devices in a mesh: ctx: 32 (over y, z), tp: 8 (over x, core).
Axes of the slice: x: 4, y: 4, z: 8, core: 2. Of those that a mesh axis runs over, the one named last changes fastest.
Arguments:
- queries: bfloat16 [2048, 8192], P('ctx', 'tp'), as said below
- new_keys: bfloat16 [2048, 1024], P('ctx', 'tp'), may hold values from -5 to 5
- new_values: bfloat16 [2048, 1024], P('ctx', 'tp'), may hold values from -5 to 5
- cache_keys: bfloat16 [8, 24576, 1024], P(None, 'ctx', 'tp'), as said below
- cache_values: bfloat16 [8, 24576, 1024], P(None, 'ctx', 'tp'), may hold values from -5 to 5
- cache_lengths: int32 [8, 32], P(None, 'ctx'), may hold values from 1 to 768, 12288 in all within a row
- turn_start: int32 [8], replicated, may hold values from 0 to 127
- out_weight: bfloat16 [8192, 4096], P('tp'), may hold values from -0.0625 to 0.0625
Outputs:
- mixed: bfloat16 [2048, 4096], P(('ctx', 'tp'))
The draws below stay inside these ranges and needn't reach their ends.
Inputs may be any that keep to these rules, and one draw needn't show every extreme that they name: `queries`: within -8 to 8. `cache_keys`: within -8 to 8. `cache_lengths`: every shard holds one filled position at least; 768 is reached in every trajectory.
All inputs are finite; a program needn't handle non-finite values.
Results may differ from the reference program's by a relative error of at most 0.022.
Values may be sent and summed in bfloat16 or wider, within the bound.
A program may use at most 128 MiB of HBM per device.

```python
import math
import jax
import jax.numpy as jnp
import numpy as np
from jax import lax

H = 64
KVH = 8
HD = 128
OUT = 4096
NEW = 256
CACHE = 24576
ROWS = 2048
TRAJ = 8
CACHE_DEV = 768
N_CTX = 32


def draw_queries(key, part):
    key = jax.random.fold_in(key, 3)
    values = jnp.clip(jax.random.normal(key, (ROWS, H * HD), jnp.float32), -5.0, 5.0)
    return values.astype(jnp.bfloat16)


def draw_cache_keys(key, part):
    key = jax.random.fold_in(key, 4)
    values = jnp.clip(jax.random.normal(key, (TRAJ, CACHE, KVH * HD), jnp.float32), -5.0, 5.0)
    return values.astype(jnp.bfloat16)


def touch_ends(result, rng, least, top_value):
    dims = result.shape
    spot = [jax.random.randint(jax.random.fold_in(rng, axis), (), 0, dims[axis]) for axis in range(len(dims))]
    result = result.at[tuple(spot)].set(least)
    longest = dims.index(max(dims))
    spot[longest] = (spot[longest] + 1) % dims[longest]
    return result.at[tuple(spot)].set(top_value)


def levels(key, shape, shards, smallest, largest):
    loudness = 1.0
    for axis_at, blocks in shards:
        heights = jax.random.uniform(jax.random.fold_in(jax.random.fold_in(key, 6), axis_at), (blocks,), jnp.float32, smallest / len(shards), largest / len(shards))
        loudness = loudness * jnp.repeat(jnp.exp(heights), shape[axis_at] // blocks).reshape((-1,) + (1,) * (len(shape) - 1 - axis_at))
    return loudness


def length_profile(number_of, total, bound, lean):
    weights = [(1 << 20) // math.isqrt(standing ** lean) + 1 for standing in range(2, number_of + 1)]
    surplus, given = total - bound - (number_of - 1), [1] * (number_of - 1)
    while surplus > 0:
        free = [i for i in range(number_of - 1) if given[i] < bound]
        whole, left = sum([weights[i] for i in free]), surplus
        for i in free:
            more = min(bound - given[i], max(1, left * weights[i] // whole), surplus)
            given[i] = given[i] + more
            surplus = surplus - more
    return np.array([bound] + given)


def uneven(rng, amount, total, reach, slope):
    if amount == 2:
        one = jax.random.randint(rng, (), max(1, total - reach), min(reach, total - 1) + 1)
        return jnp.stack([one, total - one])
    tallies = jnp.asarray(length_profile(amount, total, reach, slope), jnp.int32)
    twos = (amount - 1) // 2
    donor, sink = tallies[1:1 + 2 * twos:2], tallies[2:2 + 2 * twos:2]
    slack = jnp.minimum(donor - 1, reach - sink)
    shifted = jax.random.randint(jax.random.fold_in(rng, 1), (twos,), 0, 1 << 20) % (slack + 1)
    tallies = tallies.at[1:1 + 2 * twos:2].set(donor - shifted).at[2:2 + 2 * twos:2].set(sink + shifted)
    return tallies[jax.random.permutation(jax.random.fold_in(rng, 2), amount)]


def normal_values(stream_key, shape, width, limit, shards=(), kind=jnp.bfloat16):
    drawn = width * jax.random.normal(stream_key, shape, jnp.float32)
    if shards:
        drawn = drawn * levels(stream_key, shape, shards, -0.22, 0.18)
    return jnp.clip(drawn, -limit, limit).astype(kind)


def setup_inputs(seed: int = 0) -> dict:
    seeds = jax.random.split(jax.random.key(seed), 9)
    queries = draw_queries(jax.random.fold_in(seeds[8], 71), 0)
    new_keys = normal_values(seeds[1], (ROWS, KVH * HD), 1.0, 5.0, ((0, 32), (1, 8)))
    new_values = normal_values(seeds[2], (ROWS, KVH * HD), 1.0, 5.0, ((0, 32), (1, 8)))
    cache_keys = draw_cache_keys(jax.random.fold_in(seeds[8], 71), 0)
    cache_values = normal_values(seeds[4], (TRAJ, CACHE, KVH * HD), 1.0, 5.0, ((1, 32), (2, 8)))
    cache_lengths = jax.vmap(lambda own: uneven(own, N_CTX, CACHE // 2, CACHE_DEV, 2))(jax.random.split(seeds[5], TRAJ)).reshape((TRAJ, N_CTX)).astype(jnp.int32)
    turn_start = touch_ends(jax.random.randint(seeds[6], (TRAJ,), 0, NEW // 2), jax.random.fold_in(seeds[6], 1), 0, (NEW // 2) - 1).astype(jnp.int32)
    out_weight = normal_values(seeds[7], (H * HD, OUT), (H * HD) ** -0.5, 0.0625, ((0, 8),))
    return {"queries": queries, "new_keys": new_keys, "new_values": new_values, "cache_keys": cache_keys, "cache_values": cache_values, "cache_lengths": cache_lengths, "turn_start": turn_start, "out_weight": out_weight}


def reference(queries, new_keys, new_values, cache_keys, cache_values, cache_lengths, turn_start, out_weight):
    group_size = H // KVH
    score_scale = 1.0 / math.sqrt(HD)
    position = jnp.arange(NEW, dtype=jnp.int32)
    slot_ids = jnp.arange(CACHE, dtype=jnp.int32)

    def one_traj(traj_index):
        first_row = (traj_index * NEW).astype(jnp.int32)
        query_rows = lax.dynamic_slice_in_dim(queries, first_row, NEW, 0).reshape(NEW, KVH, group_size, HD).transpose(1, 2, 0, 3)
        fresh_keys = lax.dynamic_slice_in_dim(new_keys, first_row, NEW, 0).reshape(NEW, KVH, HD).transpose(1, 0, 2)
        fresh_values = lax.dynamic_slice_in_dim(new_values, first_row, NEW, 0).reshape(NEW, KVH, HD).transpose(1, 0, 2)
        stored_keys = lax.dynamic_index_in_dim(cache_keys, traj_index, 0, keepdims=False).reshape(CACHE, KVH, HD).transpose(1, 0, 2)
        stored_values = lax.dynamic_index_in_dim(cache_values, traj_index, 0, keepdims=False).reshape(CACHE, KVH, HD).transpose(1, 0, 2)
        shard_fill = lax.dynamic_index_in_dim(cache_lengths, traj_index, 0, keepdims=False)
        cache_ok = slot_ids % CACHE_DEV < shard_fill[slot_ids // CACHE_DEV]
        turn_begin = lax.dynamic_index_in_dim(turn_start, traj_index, 0, keepdims=False)
        new_ok = (position[None, :] <= position[:, None]) & (position[None, :] >= turn_begin)
        allowed = jnp.concatenate([jnp.broadcast_to(cache_ok[None, :], (NEW, CACHE)), new_ok], axis=1)
        key_rows = jnp.concatenate([stored_keys, fresh_keys], axis=1)
        value_rows = jnp.concatenate([stored_values, fresh_values], axis=1)

        def one_head(packed):
            head_queries, head_keys, head_values = packed
            scores = jnp.einsum('grd,nd->grn', head_queries.astype(jnp.float32), head_keys.astype(jnp.float32)) * score_scale
            scores = jnp.where(allowed[None], scores, -1e+30)
            highest = lax.optimization_barrier(jnp.max(scores, axis=-1))
            weights = jnp.where(allowed[None], jnp.exp(scores - highest[..., None]), 0.0)
            totals = lax.optimization_barrier(jnp.sum(weights, axis=-1))
            rounded = lax.optimization_barrier(weights.astype(jnp.bfloat16))
            summed = jnp.einsum('grn,nd->grd', rounded.astype(jnp.float32), head_values.astype(jnp.float32))
            return summed / totals[..., None]
        heads = lax.map(one_head, (query_rows, key_rows, value_rows))
        return heads.transpose(2, 0, 1, 3).reshape(NEW, H * HD).astype(jnp.bfloat16)
    attended = lax.map(one_traj, jnp.arange(TRAJ, dtype=jnp.int32)).reshape(ROWS, H * HD)
    return jnp.dot(attended, out_weight, preferred_element_type=jnp.float32).astype(jnp.bfloat16)
```

```python
import math

import jax
import jax.numpy as jnp
from jax import lax
from jax.experimental import pallas as pl
from jax.experimental.pallas import tpu as pltpu
from jax.sharding import PartitionSpec as P

HD = 128
GROUP = 8
NY = 4
NZ = 8
NTP = 8
SHARD = 768
HALF = SHARD // 2
HOME_ROWS = 64
QC = GROUP * HOME_ROWS
N_HOME = 4
OUT = 4096
VROWS = HD + 16
MASKED = -1e30
EXP2_SCALE = math.log2(math.e) / math.sqrt(HD)
DY = (0, 1, 3, 2)
N_COL = 2
COL = OUT // N_COL
MESH = pl.DeviceIdType.MESH


def kernel(
    q_ref, nk_ref, nv_ref, ck_ref, cv_ref, len_ref, start_ref, w_ref, out_ref,
    qst, qbuf, kbuf, vbuf, kp, vt, lst, lbuf, nkbuf, nvbuf, vtn, acc, mx,
    ost, sst, obuf, sbuf, att, wbuf, pst, rbuf,
    w_sem, kv_send, kv_recv, l_send, l_recv, q_send, q_recv,
    n_send, n_recv, o_send, o_recv, s_send, s_recv, p_send, p_recv,
):
    ctx = lax.axis_index("ctx")
    tp = lax.axis_index("tp")
    y = ctx // NZ
    z = ctx % NZ
    par = z % 2
    held = 2 * y + par
    home_par = z // 4
    home_slot = z % 4

    def at(row, col):
        return {"ctx": row * NZ + col, "tp": tp}

    def row_of(oi):
        return (y + DY[oi]) % NY

    barrier = pltpu.get_barrier_semaphore()
    n_peers = 0
    for dy in range(NY):
        for dz in range(NZ):
            if (dy == 0 and dz != 0) or (dy != 0 and dz in (0, 1, NZ - 1)):
                pl.semaphore_signal(
                    barrier, inc=1, device_id=at((y + dy) % NY, (z + dz) % NZ), device_id_type=MESH
                )
                n_peers += 1
    for d in range(1, NTP):
        pl.semaphore_signal(
            barrier, inc=1, device_id={"ctx": ctx, "tp": (tp + d) % NTP}, device_id_type=MESH
        )
        n_peers += 1

    w_copy = pltpu.make_async_copy(w_ref, wbuf, w_sem)
    own = []
    for h in range(2):
        rows = pl.ds(h * HALF, HALF)
        for kv, (src, dst) in enumerate(((ck_ref, kbuf), (cv_ref, vbuf))):
            own.append(
                pltpu.make_async_copy(
                    src.at[held, rows], dst.at[0, rows], kv_recv.at[0, h, kv]
                )
            )
    for copy in own:
        copy.start()
    w_copy.start()
    for g in range(GROUP):
        qst[pl.ds(g * HOME_ROWS, HOME_ROWS), :] = q_ref[:, pl.ds(g * HD, HD)]
    for oi in range(NY):
        row = row_of(oi)
        lst[oi, 0] = jnp.full((8, 128), len_ref[2 * row + par, 0], jnp.int32)
        lst[oi, 1] = jnp.full((8, 128), len_ref[2 * row + 1 - par, 0], jnp.int32)
    lbuf[0, 0] = lst[0, 0]

    pl.semaphore_wait(barrier, n_peers)

    def remote(src, dst, send, recv, device):
        return pltpu.make_async_remote_copy(
            src_ref=src, dst_ref=dst, send_sem=send, recv_sem=recv,
            device_id=device, device_id_type=MESH,
        )

    def q_copy(i):
        return remote(
            qst, qbuf.at[home_slot], q_send.at[i], q_recv.at[home_slot], at(y, 2 * i + home_par)
        )

    def q_local():
        return pltpu.make_async_copy(qst, qbuf.at[home_slot], q_recv.at[home_slot])

    for i in range(N_HOME):
        target = 2 * i + home_par

        @pl.when(target != z)
        def _():
            q_copy(i).start()

        @pl.when(target == z)
        def _():
            q_local().start()

    new_target = 2 * home_slot + home_par

    def n_copy(kv):
        return remote(
            (nk_ref, nv_ref)[kv], (nkbuf, nvbuf)[kv], n_send.at[kv], n_recv.at[kv], at(y, new_target)
        )

    def n_local(kv):
        return pltpu.make_async_copy((nk_ref, nv_ref)[kv], (nkbuf, nvbuf)[kv], n_recv.at[kv])

    for kv in range(2):

        @pl.when(new_target != z)
        def _():
            n_copy(kv).start()

        @pl.when(new_target == z)
        def _():
            n_local(kv).start()

    kv_copies = []
    l_copies = []
    for oi in range(NY):
        row = row_of(oi)
        for cross in range(2):
            if oi == 0 and cross == 0:
                continue
            traj = 2 * row + (1 - par if cross else par)
            for h in range(2):
                dz = 0 if not cross else (1 if h == 0 else NZ - 1)
                device = at(row, (z + dz) % NZ)
                if cross or h == 0:
                    slot = 0 if not cross else 1 + h
                    l_copies.append(
                        remote(
                            lst.at[oi, cross], lbuf.at[oi, slot],
                            l_send.at[oi, slot], l_recv.at[oi, slot], device,
                        )
                    )
                rows = pl.ds(h * HALF, HALF)
                for kv, (src, dst) in enumerate(((ck_ref, kbuf), (cv_ref, vbuf))):
                    b = 2 * oi + cross
                    kv_copies.append(
                        remote(
                            src.at[traj, rows], dst.at[b, rows],
                            kv_send.at[b, h, kv], kv_recv.at[b, h, kv], device,
                        )
                    )
    for copy in l_copies:
        copy.start()
    for copy in kv_copies:
        copy.start()

    acc[...] = jnp.zeros_like(acc)
    mx[...] = jnp.full_like(mx, MASKED)
    sst[...] = jnp.zeros_like(sst)

    for j in range(N_HOME):
        pltpu.make_async_copy(qst, qbuf.at[j], q_recv.at[j]).wait()

    def update(j, s, vt_rows):
        old = mx[j, 0:1, :]
        new = jnp.maximum(old, jnp.max(s, axis=0, keepdims=True))
        p = jnp.exp2((s - new) * EXP2_SCALE).astype(jnp.bfloat16)
        fade = jnp.exp2((old - new) * EXP2_SCALE)
        part = jnp.dot(vt_rows, p, preferred_element_type=jnp.float32)
        acc[j] = acc[j] * fade + part
        mx[j, 0:1, :] = new

    def scores(keys, j):
        return lax.dot_general(
            keys, qbuf[j], (((1,), (1,)), ((), ())), preferred_element_type=jnp.float32
        )

    position = lax.broadcasted_iota(jnp.int32, (HALF, HD), 0)
    lane_position = lax.broadcasted_iota(jnp.int32, (16, HD), 1)
    first_row = lax.broadcasted_iota(jnp.int32, (16, HD), 0) == 0

    def block(b, carry):
        oi = b // 2
        cross = b % 2
        for h in range(2):
            rows = pl.ds(h * HALF, HALF)
            slot = cross * (1 + h)

            if h == 0:

                @pl.when(b > 0)
                def _():
                    pltpu.make_async_copy(
                        lst.at[0, 0], lbuf.at[oi, slot], l_recv.at[oi, slot]
                    ).wait()

            else:

                @pl.when(cross == 1)
                def _():
                    pltpu.make_async_copy(
                        lst.at[0, 0], lbuf.at[oi, slot], l_recv.at[oi, slot]
                    ).wait()

            pltpu.make_async_copy(
                ck_ref.at[0, rows], kbuf.at[b, rows], kv_recv.at[b, h, 0]
            ).wait()
            pltpu.make_async_copy(
                cv_ref.at[0, rows], vbuf.at[b, rows], kv_recv.at[b, h, 1]
            ).wait()
        for h in range(2):
            rows = pl.ds(h * HALF, HALF)
            fill = lbuf[oi, cross * (1 + h)]
            ok = position + h * HALF < fill[0:1, :]
            spare = kbuf[0, 0:16, :].astype(jnp.float32)[0:1, :]
            keys = kbuf[b, rows, :].astype(jnp.float32)
            kp[rows, :] = jnp.where(ok, keys, spare).astype(jnp.bfloat16)
            values = jnp.where(ok, vbuf[b, rows, :].astype(jnp.float32), 0.0)
            vt[0:HD, rows] = values.T.astype(jnp.bfloat16)
            for g in range(HALF // HD):
                first = h * HALF + g * HD
                counted = first_row & (lane_position + first < fill[0:1, :])
                vt[HD:VROWS, pl.ds(first, HD)] = jnp.where(counted, 1.0, 0.0).astype(jnp.bfloat16)

        def chunk(j, carry):
            update(j, scores(kp[...], j), vt[...])
            return carry

        return lax.fori_loop(0, N_HOME, chunk, carry)

    lax.fori_loop(0, 1, block, 0)

    for kv in range(2):
        pltpu.make_async_copy(
            (nk_ref, nv_ref)[kv], (nkbuf, nvbuf)[kv], n_recv.at[kv]
        ).wait()
    vtn[0:HD, :] = nvbuf[...].astype(jnp.float32).T.astype(jnp.bfloat16)
    ones = lax.broadcasted_iota(jnp.int32, (16, HOME_ROWS), 0) == 0
    vtn[HD:VROWS, :] = jnp.where(ones, 1.0, 0.0).astype(jnp.bfloat16)
    key_pos = (z // 2) * HOME_ROWS + lax.broadcasted_iota(jnp.int32, (HOME_ROWS, QC), 0)
    row_pos = lax.broadcasted_iota(jnp.int32, (HOME_ROWS, QC), 1) % HOME_ROWS
    begun = key_pos >= start_ref[held]

    def new_chunk(j, carry):
        ok = begun & (key_pos <= row_pos + j * HOME_ROWS)
        update(j, jnp.where(ok, scores(nkbuf[...], j), MASKED), vtn[...])
        return carry

    lax.fori_loop(0, N_HOME, new_chunk, 0)

    lax.fori_loop(1, 2 * NY, block, 0)

    def o_copy(j):
        device = at(y, 4 * par + j)
        return (
            remote(ost.at[j], obuf.at[z // 2], o_send.at[j], o_recv.at[z // 2], device),
            remote(sst.at[j], sbuf.at[z // 2], s_send.at[j], s_recv.at[z // 2], device),
        )

    def o_local(j):
        return (
            pltpu.make_async_copy(ost.at[j], obuf.at[z // 2], o_recv.at[z // 2]),
            pltpu.make_async_copy(sst.at[j], sbuf.at[z // 2], s_recv.at[z // 2]),
        )

    for j in range(N_HOME):
        ost[j] = acc[j, 0:HD, :].astype(jnp.bfloat16)
        sst[j, 0:1, :] = mx[j, 0:1, :]
        sst[j, 1:2, :] = acc[j, HD : HD + 1, :]

        @pl.when(4 * par + j != z)
        def _():
            for copy in o_copy(j):
                copy.start()

        @pl.when(4 * par + j == z)
        def _():
            for copy in o_local(j):
                copy.start()

    w_copy.wait()
    for i in range(N_HOME):
        pltpu.make_async_copy(ost.at[0], obuf.at[i], o_recv.at[i]).wait()
        pltpu.make_async_copy(sst.at[0], sbuf.at[i], s_recv.at[i]).wait()

    top = sbuf[0, 0:1, :]
    for i in range(1, N_HOME):
        top = jnp.maximum(top, sbuf[i, 0:1, :])
    total = jnp.zeros((1, QC), jnp.float32)
    summed = jnp.zeros((HD, QC), jnp.float32)
    for i in range(N_HOME):
        factor = jnp.exp2((sbuf[i, 0:1, :] - top) * EXP2_SCALE)
        total = total + factor * sbuf[i, 1:2, :]
        summed = summed + factor * obuf[i].astype(jnp.float32)
    attended = (summed / total).T
    for g in range(GROUP):
        att[:, pl.ds(g * HD, HD)] = attended[g * HOME_ROWS : (g + 1) * HOME_ROWS].astype(jnp.bfloat16)

    def p_copy(c, d):
        to = (tp + d) % NTP
        return remote(
            pst.at[c, to], rbuf.at[c, tp], p_send.at[c, d], p_recv.at[c, tp], {"ctx": ctx, "tp": to}
        )

    for c in range(N_COL):
        for g in range(2):
            half = c * COL + g * (COL // 2)
            prod = jnp.dot(
                att[...], wbuf[:, pl.ds(half, COL // 2)], preferred_element_type=jnp.float32
            )
            for t in range(NTP):
                pst[c, t, pl.ds(g * 8, 8), :] = prod[t * 8 : (t + 1) * 8, :].astype(jnp.bfloat16)
        for d in range(1, NTP):
            p_copy(c, d).start()

    for c in range(N_COL):
        sums = pst[c, tp].astype(jnp.float32)
        for d in range(1, NTP):
            source = (tp + d) % NTP
            pltpu.make_async_copy(pst.at[c, 0], rbuf.at[c, source], p_recv.at[c, source]).wait()
            sums = sums + rbuf[c, source].astype(jnp.float32)
        for g in range(2):
            out_ref[:, pl.ds(c * COL + g * (COL // 2), COL // 2)] = sums[g * 8 : (g + 1) * 8].astype(
                jnp.bfloat16
            )

    for i in range(N_HOME):

        @pl.when(2 * i + home_par != z)
        def _():
            q_copy(i).wait_send()

    for kv in range(2):

        @pl.when(new_target != z)
        def _():
            n_copy(kv).wait_send()

    for copy in l_copies + kv_copies:
        copy.wait_send()
    for j in range(N_HOME):

        @pl.when(4 * par + j != z)
        def _():
            for copy in o_copy(j):
                copy.wait_send()

    for c in range(N_COL):
        for d in range(1, NTP):
            p_copy(c, d).wait_send()


def on_device(queries, new_keys, new_values, cache_keys, cache_values, lengths, turn_start, out_weight):
    vmem = pl.BlockSpec(memory_space=pltpu.VMEM)
    smem = pl.BlockSpec(memory_space=pltpu.SMEM)
    hbm = pl.BlockSpec(memory_space=pl.ANY)
    bf16, f32, i32 = jnp.bfloat16, jnp.float32, jnp.int32
    dma = pltpu.SemaphoreType.DMA
    return pl.pallas_call(
        kernel,
        out_shape=jax.ShapeDtypeStruct((HOME_ROWS // NTP, OUT), bf16),
        in_specs=[vmem, vmem, vmem, hbm, hbm, smem, smem, hbm],
        out_specs=vmem,
        scratch_shapes=[
            pltpu.VMEM((QC, HD), bf16),
            pltpu.VMEM((N_HOME, QC, HD), bf16),
            pltpu.VMEM((2 * NY, SHARD, HD), bf16),
            pltpu.VMEM((2 * NY, SHARD, HD), bf16),
            pltpu.VMEM((SHARD, HD), bf16),
            pltpu.VMEM((VROWS, SHARD), bf16),
            pltpu.VMEM((NY, 2, 8, 128), i32),
            pltpu.VMEM((NY, 3, 8, 128), i32),
            pltpu.VMEM((HOME_ROWS, HD), bf16),
            pltpu.VMEM((HOME_ROWS, HD), bf16),
            pltpu.VMEM((VROWS, HOME_ROWS), bf16),
            pltpu.VMEM((N_HOME, VROWS, QC), f32),
            pltpu.VMEM((N_HOME, 8, QC), f32),
            pltpu.VMEM((N_HOME, HD, QC), bf16),
            pltpu.VMEM((N_HOME, 8, QC), f32),
            pltpu.VMEM((N_HOME, HD, QC), bf16),
            pltpu.VMEM((N_HOME, 8, QC), f32),
            pltpu.VMEM((HOME_ROWS, GROUP * HD), bf16),
            pltpu.VMEM((GROUP * HD, OUT), bf16),
            pltpu.VMEM((N_COL, NTP, 16, COL // 2), bf16),
            pltpu.VMEM((N_COL, NTP, 16, COL // 2), bf16),
            dma,
            dma((2 * NY, 2, 2)),
            dma((2 * NY, 2, 2)),
            dma((NY, 3)),
            dma((NY, 3)),
            dma((N_HOME,)),
            dma((N_HOME,)),
            dma((2,)),
            dma((2,)),
            dma((N_HOME,)),
            dma((N_HOME,)),
            dma((N_HOME,)),
            dma((N_HOME,)),
            dma((N_COL, NTP)),
            dma((N_COL, NTP)),
        ],
        compiler_params=pltpu.CompilerParams(
            collective_id=0, has_side_effects=True, vmem_limit_bytes=48 << 20
        ),
        name="attend_project",
    )(queries, new_keys, new_values, cache_keys, cache_values, lengths, turn_start, out_weight)


def solution(mesh):
    in_specs = (
        P("ctx", "tp"),
        P("ctx", "tp"),
        P("ctx", "tp"),
        P(None, "ctx", "tp"),
        P(None, "ctx", "tp"),
        P(None, "ctx"),
        P(),
        P("tp", None),
    )
    return jax.shard_map(
        on_device, mesh=mesh, in_specs=in_specs, out_specs=P(("ctx", "tp"), None), check_vma=False
    )
```

```python
import math

import jax
import jax.numpy as jnp
from jax import lax
from jax.experimental import pallas as pl
from jax.experimental.pallas import tpu as pltpu
from jax.sharding import PartitionSpec as P

HD = 128
GROUP = 8
NY = 4
NZ = 8
NTP = 8
NX = 4
SHARD = 768
HALF = SHARD // 2
HOME_ROWS = 64
QC = GROUP * HOME_ROWS
N_HOME = 4
GL = QC // 2
OUT = 4096
VROWS = HD + 16
MASKED = -1e30
EXP2_SCALE = math.log2(math.e) / math.sqrt(HD)
DY = (0, 1, 3, 2)
N_COL = 4
COL = OUT // N_COL
MESH = pl.DeviceIdType.MESH


def kernel(
    q_hbm, nk_ref, nv_ref, ck_ref, cv_ref, len_hbm, start_hbm, w_ref, out_ref,
    q_ref, len_ref, start_ref, qst, qbuf, kbuf, vbuf, kp, vt, sa, sb, lst, lbuf, nkbuf, nvbuf, vtn, acc, mx,
    ost, sst, obuf, sbuf, att, proj, wbuf, pst, cbuf, xst, rbuf,
    in_sem, w_sem, kv_send, kv_recv, l_send, l_recv, q_send, q_recv,
    n_send, n_recv, o_send, o_recv, s_send, s_recv, c_send, c_recv, p_send, p_recv,
):
    ctx = lax.axis_index("ctx")
    tp = lax.axis_index("tp")
    y = ctx // NZ
    z = ctx % NZ
    x = tp // 2
    core = tp % 2
    par = z % 2
    held = 2 * y + par
    home_par = z // 4
    home_slot = z % 4

    def at(row, col):
        return {"ctx": row * NZ + col, "tp": tp}

    sibling = {"ctx": ctx, "tp": tp // 2 * 2 + 1 - core}

    def across(d):
        return {"ctx": ctx, "tp": (x + d) % NX * 2 + core}

    def row_of(oi):
        return (y + DY[oi]) % NY

    inputs = [
        pltpu.make_async_copy(src, dst, in_sem.at[i])
        for i, (src, dst) in enumerate(((q_hbm, q_ref), (len_hbm, len_ref), (start_hbm, start_ref)))
    ]
    for copy in inputs:
        copy.start()

    barrier = pltpu.get_barrier_semaphore()
    n_peers = 0
    for dy in range(NY):
        for dz in range(NZ):
            if (dy == 0 and dz != 0) or (dy != 0 and dz in (0, 1, NZ - 1)):
                pl.semaphore_signal(
                    barrier, inc=1, device_id=at((y + dy) % NY, (z + dz) % NZ), device_id_type=MESH
                )
                n_peers += 1
    for peer in [sibling] + [across(d) for d in range(1, NX)]:
        pl.semaphore_signal(barrier, inc=1, device_id=peer, device_id_type=MESH)
        n_peers += 1

    w_copy = pltpu.make_async_copy(w_ref, wbuf, w_sem)
    own = []
    for h in range(2):
        rows = pl.ds(h * HALF, HALF)
        for kv, (src, dst) in enumerate(((ck_ref, kbuf), (cv_ref, vbuf))):
            own.append(
                pltpu.make_async_copy(
                    src.at[held, rows], dst.at[0, rows], kv_recv.at[0, h, kv]
                )
            )
    for copy in own:
        copy.start()
    w_copy.start()
    for copy in inputs:
        copy.wait()
    for g in range(GROUP):
        qst[pl.ds(g * HOME_ROWS, HOME_ROWS), :] = q_ref[:, pl.ds(g * HD, HD)]
    for oi in range(NY):
        row = row_of(oi)
        lst[oi, 0] = jnp.full((8, 128), len_ref[0, 2 * row + par], jnp.int32)
        lst[oi, 1] = jnp.full((8, 128), len_ref[0, 2 * row + 1 - par], jnp.int32)
    lbuf[0, 0] = lst[0, 0]

    pl.semaphore_wait(barrier, n_peers)

    def remote(src, dst, send, recv, device):
        return pltpu.make_async_remote_copy(
            src_ref=src, dst_ref=dst, send_sem=send, recv_sem=recv,
            device_id=device, device_id_type=MESH,
        )

    kv_first = []
    kv_copies = []
    l_copies = []
    for oi in range(NY):
        row = row_of(oi)
        for cross in range(2):
            if oi == 0 and cross == 0:
                continue
            traj = 2 * row + (1 - par if cross else par)
            for h in range(2):
                dz = 0 if not cross else (1 if h == 0 else NZ - 1)
                device = at(row, (z + dz) % NZ)
                if cross or h == 0:
                    slot = 0 if not cross else 1 + h
                    l_copies.append(
                        remote(
                            lst.at[oi, cross], lbuf.at[oi, slot],
                            l_send.at[oi, slot], l_recv.at[oi, slot], device,
                        )
                    )
                rows = pl.ds(h * HALF, HALF)
                for kv, (src, dst) in enumerate(((ck_ref, kbuf), (cv_ref, vbuf))):
                    b = 2 * oi + cross
                    copy = remote(
                        src.at[traj, rows], dst.at[b, rows],
                        kv_send.at[b, h, kv], kv_recv.at[b, h, kv], device,
                    )
                    (kv_first if oi in (1, 2) and not cross else kv_copies).append(copy)
    for copy in kv_first:
        copy.start()

    def q_copy(i):
        return remote(
            qst, qbuf.at[home_slot], q_send.at[i], q_recv.at[home_slot], at(y, 2 * i + home_par)
        )

    def q_local():
        return pltpu.make_async_copy(qst, qbuf.at[home_slot], q_recv.at[home_slot])

    for i in range(N_HOME):
        target = 2 * i + home_par

        @pl.when(target != z)
        def _():
            q_copy(i).start()

        @pl.when(target == z)
        def _():
            q_local().start()

    new_target = 2 * home_slot + home_par

    def n_copy(kv):
        return remote(
            (nk_ref, nv_ref)[kv], (nkbuf, nvbuf)[kv], n_send.at[kv], n_recv.at[kv], at(y, new_target)
        )

    def n_local(kv):
        return pltpu.make_async_copy((nk_ref, nv_ref)[kv], (nkbuf, nvbuf)[kv], n_recv.at[kv])

    for kv in range(2):

        @pl.when(new_target != z)
        def _():
            n_copy(kv).start()

        @pl.when(new_target == z)
        def _():
            n_local(kv).start()

    for copy in l_copies + kv_copies:
        copy.start()

    acc[...] = jnp.zeros_like(acc)
    mx[...] = jnp.full_like(mx, MASKED)
    sst[...] = jnp.zeros_like(sst)

    for j in range(N_HOME):
        pltpu.make_async_copy(qst, qbuf.at[j], q_recv.at[j]).wait()

    def scores(keys, j, held_scores):
        s = lax.dot_general(
            keys, qbuf[j], (((1,), (1,)), ((), ())), preferred_element_type=jnp.float32
        )
        held_scores[...] = s
        old = mx[j, 0:1, :]
        new = jnp.maximum(old, jnp.max(s, axis=0, keepdims=True))
        mx[j, 0:1, :] = new
        return old, new

    def update(j, s, old, new, vt_rows):
        p = jnp.exp2((s - new) * EXP2_SCALE).astype(jnp.bfloat16)
        fade = jnp.exp2((old - new) * EXP2_SCALE)
        part = jnp.dot(vt_rows, p, preferred_element_type=jnp.float32)
        acc[j] = acc[j] * fade + part

    def sweep(first, count, done=None):
        rows = pl.ds(first, count)
        buffers = (sa.at[pl.ds(0, count)], sb.at[pl.ds(0, count)])
        state = scores(kp[rows, :], 0, buffers[0])
        for j in range(N_HOME):
            ahead = scores(kp[rows, :], j + 1, buffers[(j + 1) % 2]) if j + 1 < N_HOME else None
            update(j, buffers[j % 2][...], *state, vt[:, rows])
            if done is not None:
                done(j)
            state = ahead

    position = lax.broadcasted_iota(jnp.int32, (HALF, HD), 0)
    lane_position = lax.broadcasted_iota(jnp.int32, (16, HD), 1)
    first_row = lax.broadcasted_iota(jnp.int32, (16, HD), 0) == 0

    def arrive(b, at_key):
        oi = b // 2
        cross = b % 2
        for h in range(2):
            rows = pl.ds(h * HALF, HALF)
            slot = cross * (1 + h)
            if b > 0 and (cross or h == 0):
                pltpu.make_async_copy(lst.at[0, 0], lbuf.at[oi, slot], l_recv.at[oi, slot]).wait()
            pltpu.make_async_copy(ck_ref.at[0, rows], kbuf.at[b, rows], kv_recv.at[b, h, 0]).wait()
            pltpu.make_async_copy(cv_ref.at[0, rows], vbuf.at[b, rows], kv_recv.at[b, h, 1]).wait()
        spare = kbuf[0, 0:16, :].astype(jnp.float32)[0:1, :]
        for h in range(2):
            rows = pl.ds(h * HALF, HALF)
            put = pl.ds(at_key + h * HALF, HALF)
            fill = lbuf[oi, cross * (1 + h)]
            ok = position + h * HALF < fill[0:1, :]
            keys = kbuf[b, rows, :].astype(jnp.float32)
            kp[put, :] = jnp.where(ok, keys, spare).astype(jnp.bfloat16)
            values = jnp.where(ok, vbuf[b, rows, :].astype(jnp.float32), 0.0)
            vt[0:HD, put] = values.T.astype(jnp.bfloat16)
            for g in range(HALF // HD):
                first = h * HALF + g * HD
                counted = first_row & (lane_position + first < fill[0:1, :])
                vt[HD:VROWS, pl.ds(at_key + first, HD)] = jnp.where(counted, 1.0, 0.0).astype(
                    jnp.bfloat16
                )

    for oi in range(NY - 1):
        arrive(2 * oi, 0)
        arrive(2 * oi + 1, SHARD)
        sweep(0, 2 * SHARD)

    for kv in range(2):
        pltpu.make_async_copy(
            (nk_ref, nv_ref)[kv], (nkbuf, nvbuf)[kv], n_recv.at[kv]
        ).wait()
    vtn[0:HD, :] = nvbuf[...].astype(jnp.float32).T.astype(jnp.bfloat16)
    ones = lax.broadcasted_iota(jnp.int32, (16, HOME_ROWS), 0) == 0
    vtn[HD:VROWS, :] = jnp.where(ones, 1.0, 0.0).astype(jnp.bfloat16)
    key_pos = (z // 2) * HOME_ROWS + lax.broadcasted_iota(jnp.int32, (HOME_ROWS, QC), 0)
    row_pos = lax.broadcasted_iota(jnp.int32, (HOME_ROWS, QC), 1) % HOME_ROWS
    begun = key_pos >= start_ref[held]
    for j in range(N_HOME):
        s = lax.dot_general(
            nkbuf[...], qbuf[j], (((1,), (1,)), ((), ())), preferred_element_type=jnp.float32
        )
        s = jnp.where(begun & (key_pos <= row_pos + j * HOME_ROWS), s, MASKED)
        old = mx[j, 0:1, :]
        new = jnp.maximum(old, jnp.max(s, axis=0, keepdims=True))
        mx[j, 0:1, :] = new
        update(j, s, old, new, vtn[...])

    arrive(2 * NY - 2, 0)
    sweep(0, SHARD)
    arrive(2 * NY - 1, 0)

    def o_pairs(j, g):
        me = z // 2
        return (
            (ost.at[j, g], obuf.at[me, g], o_send.at[j, g], o_recv.at[me, g]),
            (sst.at[j, g], sbuf.at[me, g], s_send.at[j, g], s_recv.at[me, g]),
        )

    def send_partial(j, g):
        for i in range(GL // 128):
            lanes = pl.ds(g * GL + i * 128, 128)
            sst[j, g, i : i + 1, :] = mx[j, 0:1, lanes]
            sst[j, g, 4 + i : 5 + i, :] = acc[j, HD : HD + 1, lanes]
        ost[j, g] = acc[j, 0:HD, pl.ds(g * GL, GL)].astype(jnp.bfloat16)

        @pl.when(4 * par + j != z)
        def _():
            for src, dst, send, recv in o_pairs(j, g):
                remote(src, dst, send, recv, at(y, 4 * par + j)).start()

        @pl.when(4 * par + j == z)
        def _():
            for src, dst, send, recv in o_pairs(j, g):
                pltpu.make_async_copy(src, dst, recv).start()

    sweep(0, SHARD, lambda j: send_partial(j, 0))
    for j in range(N_HOME):
        send_partial(j, 1)

    w_copy.wait()

    def attend_group(g):
        for i in range(N_HOME):
            pltpu.make_async_copy(ost.at[0, g], obuf.at[i, g], o_recv.at[i, g]).wait()
            pltpu.make_async_copy(sst.at[0, g], sbuf.at[i, g], s_recv.at[i, g]).wait()

        def stat(i, first):
            rows = [sbuf[i, g, first + n : first + n + 1, :] for n in range(GL // 128)]
            return jnp.concatenate(rows, axis=1)

        highest = [stat(i, 0) for i in range(N_HOME)]
        top = highest[0]
        for i in range(1, N_HOME):
            top = jnp.maximum(top, highest[i])
        total = jnp.zeros((1, GL), jnp.float32)
        summed = jnp.zeros((HD, GL), jnp.float32)
        for i in range(N_HOME):
            factor = jnp.exp2((highest[i] - top) * EXP2_SCALE)
            total = total + factor * stat(i, 4)
            summed = summed + factor * obuf[i, g].astype(jnp.float32)
        attended = (summed / total).T
        for n in range(GL // HOME_ROWS):
            att[g, :, pl.ds(n * HD, HD)] = attended[n * HOME_ROWS : (n + 1) * HOME_ROWS].astype(
                jnp.bfloat16
            )

    depth = GROUP * HD // 2
    attend_group(0)
    for c in range(2 * N_COL):
        cols = pl.ds(c * (COL // 2), COL // 2)
        proj[:, cols] = jnp.dot(
            att[0], wbuf[pl.ds(0, depth), cols], preferred_element_type=jnp.float32
        )
    attend_group(1)

    def c_copy(c):
        return remote(
            pst.at[c, 1 - core], cbuf.at[c], c_send.at[c], c_recv.at[c], sibling
        )

    def p_copy(c, d):
        to = (x + d) % NX
        return remote(
            xst.at[c, to], rbuf.at[c, x], p_send.at[c, d], p_recv.at[c, x], across(d)
        )

    def project(c):
        for g in range(2):
            cols = pl.ds(c * COL + g * (COL // 2), COL // 2)
            prod = proj[:, cols] + jnp.dot(
                att[1], wbuf[pl.ds(depth, depth), cols], preferred_element_type=jnp.float32
            )
            for t in range(NTP):
                pst[c, t % 2, t // 2, pl.ds(g * 8, 8), :] = prod[t * 8 : (t + 1) * 8, :].astype(
                    jnp.bfloat16
                )
        c_copy(c).start()

    def to_owners(c):
        pltpu.make_async_copy(pst.at[c, 0], cbuf.at[c], c_recv.at[c]).wait()
        xst[c] = (pst[c, core].astype(jnp.float32) + cbuf[c].astype(jnp.float32)).astype(jnp.bfloat16)
        for d in range(1, NX):
            p_copy(c, d).start()

    project(0)
    for c in range(1, N_COL):
        project(c)
        to_owners(c - 1)
    to_owners(N_COL - 1)

    for c in range(N_COL):
        sums = xst[c, x].astype(jnp.float32)
        for d in range(1, NX):
            source = (x + d) % NX
            pltpu.make_async_copy(xst.at[c, 0], rbuf.at[c, source], p_recv.at[c, source]).wait()
            sums = sums + rbuf[c, source].astype(jnp.float32)
        for g in range(2):
            out_ref[:, pl.ds(c * COL + g * (COL // 2), COL // 2)] = sums[g * 8 : (g + 1) * 8].astype(
                jnp.bfloat16
            )

    for i in range(N_HOME):

        @pl.when(2 * i + home_par != z)
        def _():
            q_copy(i).wait_send()

    for kv in range(2):

        @pl.when(new_target != z)
        def _():
            n_copy(kv).wait_send()

    for copy in kv_first + l_copies + kv_copies:
        copy.wait_send()
    for j in range(N_HOME):

        @pl.when(4 * par + j != z)
        def _():
            for g in range(2):
                for src, dst, send, recv in o_pairs(j, g):
                    remote(src, dst, send, recv, at(y, 4 * par + j)).wait_send()

    for c in range(N_COL):
        c_copy(c).wait_send()
        for d in range(1, NX):
            p_copy(c, d).wait_send()


def on_device(queries, new_keys, new_values, cache_keys, cache_values, lengths, turn_start, out_weight):
    vmem = pl.BlockSpec(memory_space=pltpu.VMEM)
    hbm = pl.BlockSpec(memory_space=pl.ANY)
    bf16, f32, i32 = jnp.bfloat16, jnp.float32, jnp.int32
    dma = pltpu.SemaphoreType.DMA
    return pl.pallas_call(
        kernel,
        out_shape=jax.ShapeDtypeStruct((HOME_ROWS // NTP, OUT), bf16),
        in_specs=[hbm] * 8,
        out_specs=vmem,
        scratch_shapes=[
            pltpu.VMEM((HOME_ROWS, GROUP * HD), bf16),
            pltpu.SMEM((1, 8), i32),
            pltpu.SMEM((8,), i32),
            pltpu.VMEM((QC, HD), bf16),
            pltpu.VMEM((N_HOME, QC, HD), bf16),
            pltpu.VMEM((2 * NY, SHARD, HD), bf16),
            pltpu.VMEM((2 * NY, SHARD, HD), bf16),
            pltpu.VMEM((2 * SHARD, HD), bf16),
            pltpu.VMEM((VROWS, 2 * SHARD), bf16),
            pltpu.VMEM((2 * SHARD, QC), f32),
            pltpu.VMEM((2 * SHARD, QC), f32),
            pltpu.VMEM((NY, 2, 8, 128), i32),
            pltpu.VMEM((NY, 3, 8, 128), i32),
            pltpu.VMEM((HOME_ROWS, HD), bf16),
            pltpu.VMEM((HOME_ROWS, HD), bf16),
            pltpu.VMEM((VROWS, HOME_ROWS), bf16),
            pltpu.VMEM((N_HOME, VROWS, QC), f32),
            pltpu.VMEM((N_HOME, 8, QC), f32),
            pltpu.VMEM((N_HOME, 2, HD, GL), bf16),
            pltpu.VMEM((N_HOME, 2, 8, 128), f32),
            pltpu.VMEM((N_HOME, 2, HD, GL), bf16),
            pltpu.VMEM((N_HOME, 2, 8, 128), f32),
            pltpu.VMEM((2, HOME_ROWS, GROUP * HD // 2), bf16),
            pltpu.VMEM((HOME_ROWS, OUT), f32),
            pltpu.VMEM((GROUP * HD, OUT), bf16),
            pltpu.VMEM((N_COL, 2, NX, 16, COL // 2), bf16),
            pltpu.VMEM((N_COL, NX, 16, COL // 2), bf16),
            pltpu.VMEM((N_COL, NX, 16, COL // 2), bf16),
            pltpu.VMEM((N_COL, NX, 16, COL // 2), bf16),
            dma((3,)),
            dma,
            dma((2 * NY, 2, 2)),
            dma((2 * NY, 2, 2)),
            dma((NY, 3)),
            dma((NY, 3)),
            dma((N_HOME,)),
            dma((N_HOME,)),
            dma((2,)),
            dma((2,)),
            dma((N_HOME, 2)),
            dma((N_HOME, 2)),
            dma((N_HOME, 2)),
            dma((N_HOME, 2)),
            dma((N_COL,)),
            dma((N_COL,)),
            dma((N_COL, NX)),
            dma((N_COL, NX)),
        ],
        compiler_params=pltpu.CompilerParams(
            collective_id=0, has_side_effects=True, vmem_limit_bytes=60 << 20
        ),
        name="attend_project",
    )(queries, new_keys, new_values, cache_keys, cache_values, lengths.T, turn_start, out_weight)


def solution(mesh):
    in_specs = (
        P("ctx", "tp"),
        P("ctx", "tp"),
        P("ctx", "tp"),
        P(None, "ctx", "tp"),
        P(None, "ctx", "tp"),
        P(None, "ctx"),
        P(),
        P("tp", None),
    )
    return jax.shard_map(
        on_device, mesh=mesh, in_specs=in_specs, out_specs=P(("ctx", "tp"), None), check_vma=False
    )
```

```python
import math

import jax
import jax.numpy as jnp
from jax import lax
from jax.experimental import pallas as pl
from jax.experimental.pallas import tpu as pltpu
from jax.sharding import PartitionSpec as P

HD = 128
GROUP = 8
NY = 4
NZ = 8
NTP = 8
NX = 4
SHARD = 768
HALF = SHARD // 2
HOME_ROWS = 64
QC = GROUP * HOME_ROWS
N_HOME = 4
GL = QC // 2
OUT = 4096
VROWS = HD + 16
MASKED = -1e30
EXP2_SCALE = math.log2(math.e) / math.sqrt(HD)
DY = (0, 1, 3, 2)
N_COL = 4
COL = OUT // N_COL
MESH = pl.DeviceIdType.MESH
ORDER = (2, 4, 1, -1, -2, -3, -4, 3, 5, 7, 6)


def kernel(
    q_hbm, nk_ref, nv_ref, ck_ref, cv_ref, len_hbm, start_hbm, w_ref, out_ref,
    q_ref, len_ref, start_ref, qst, qbuf, kbuf, vbuf, kp, vt, sa, sb, lst, lbuf, nkbuf, nvbuf, vtn, acc, mx,
    ost, sst, obuf, sbuf, att, proj, wbuf, pst, cbuf, xst, rbuf,
    in_sem, w_sem, kv_send, kv_recv, l_send, l_recv, q_send, q_recv,
    n_send, n_recv, o_send, o_recv, s_send, s_recv, c_send, c_recv, p_send, p_recv,
):
    ctx = lax.axis_index("ctx")
    tp = lax.axis_index("tp")
    y = ctx // NZ
    z = ctx % NZ
    x = tp // 2
    core = tp % 2
    par = z % 2
    held = 2 * y + par
    home_par = z // 4
    home_slot = z % 4

    def at(row, col):
        return {"ctx": row * NZ + col, "tp": tp}

    sibling = {"ctx": ctx, "tp": tp // 2 * 2 + 1 - core}

    def across(d):
        return {"ctx": ctx, "tp": (x + d) % NX * 2 + core}

    def row_of(oi):
        return (y + DY[oi]) % NY

    inputs = [
        pltpu.make_async_copy(src, dst, in_sem.at[i])
        for i, (src, dst) in enumerate(((q_hbm, q_ref), (len_hbm, len_ref), (start_hbm, start_ref)))
    ]
    for copy in inputs:
        copy.start()

    barrier = pltpu.get_barrier_semaphore()
    n_peers = 0
    for dy in range(NY):
        for dz in range(NZ):
            if (dy == 0 and dz != 0) or (dy != 0 and dz in (0, 1, NZ - 1)):
                pl.semaphore_signal(
                    barrier, inc=1, device_id=at((y + dy) % NY, (z + dz) % NZ), device_id_type=MESH
                )
                n_peers += 1
    for peer in [sibling] + [across(d) for d in range(1, NX)]:
        pl.semaphore_signal(barrier, inc=1, device_id=peer, device_id_type=MESH)
        n_peers += 1

    w_copy = pltpu.make_async_copy(w_ref, wbuf, w_sem)
    own = []
    for h in range(2):
        rows = pl.ds(h * HALF, HALF)
        for kv, (src, dst) in enumerate(((ck_ref, kbuf), (cv_ref, vbuf))):
            own.append(
                pltpu.make_async_copy(
                    src.at[held, rows], dst.at[0, rows], kv_recv.at[0, h, kv]
                )
            )
    for copy in own:
        copy.start()
    w_copy.start()
    for copy in inputs:
        copy.wait()
    for g in range(GROUP):
        qst[pl.ds(g * HOME_ROWS, HOME_ROWS), :] = q_ref[:, pl.ds(g * HD, HD)]
    for oi in range(NY):
        row = row_of(oi)
        lst[oi, 0] = jnp.full((8, 128), len_ref[0, 2 * row + par], jnp.int32)
        lst[oi, 1] = jnp.full((8, 128), len_ref[0, 2 * row + 1 - par], jnp.int32)
    lbuf[0, 0] = lst[0, 0]

    pl.semaphore_wait(barrier, n_peers)

    def remote(src, dst, send, recv, device):
        return pltpu.make_async_remote_copy(
            src_ref=src, dst_ref=dst, send_sem=send, recv_sem=recv,
            device_id=device, device_id_type=MESH,
        )

    by_block = {}
    l_copies = []
    for oi in range(NY):
        row = row_of(oi)
        for cross in range(2):
            if oi == 0 and cross == 0:
                continue
            traj = 2 * row + (1 - par if cross else par)
            for h in range(2):
                dz = 0 if not cross else (1 if h == 0 else NZ - 1)
                device = at(row, (z + dz) % NZ)
                if cross or h == 0:
                    slot = 0 if not cross else 1 + h
                    l_copies.append(
                        remote(
                            lst.at[oi, cross], lbuf.at[oi, slot],
                            l_send.at[oi, slot], l_recv.at[oi, slot], device,
                        )
                    )
                rows = pl.ds(h * HALF, HALF)
                for kv, (src, dst) in enumerate(((ck_ref, kbuf), (cv_ref, vbuf))):
                    b = 2 * oi + cross
                    copy = remote(
                        src.at[traj, rows], dst.at[b, rows],
                        kv_send.at[b, h, kv], kv_recv.at[b, h, kv], device,
                    )
                    by_block.setdefault(2 * oi + cross, []).append(copy)
    def q_copy(i):
        return remote(
            qst, qbuf.at[home_slot], q_send.at[i], q_recv.at[home_slot], at(y, 2 * i + home_par)
        )

    def q_local():
        return pltpu.make_async_copy(qst, qbuf.at[home_slot], q_recv.at[home_slot])

    def send_queries(i):
        target = 2 * i + home_par

        @pl.when(target != z)
        def _():
            q_copy(i).start()

        @pl.when(target == z)
        def _():
            q_local().start()

    new_target = 2 * home_slot + home_par

    def n_copy(kv):
        return remote(
            (nk_ref, nv_ref)[kv], (nkbuf, nvbuf)[kv], n_send.at[kv], n_recv.at[kv], at(y, new_target)
        )

    def n_local(kv):
        return pltpu.make_async_copy((nk_ref, nv_ref)[kv], (nkbuf, nvbuf)[kv], n_recv.at[kv])

    for kv in range(2):

        @pl.when(new_target != z)
        def _():
            n_copy(kv).start()

        @pl.when(new_target == z)
        def _():
            n_local(kv).start()

    for copy in l_copies:
        copy.start()

    for item in ORDER:
        if item < 0:
            send_queries(-1 - item)
        else:
            for copy in by_block[item]:
                copy.start()

    acc[...] = jnp.zeros_like(acc)
    mx[...] = jnp.full_like(mx, MASKED)
    sst[...] = jnp.zeros_like(sst)

    chunks = list(range(N_HOME))

    def queries_here(k):
        pltpu.make_async_copy(qst, qbuf.at[chunks[k]], q_recv.at[chunks[k]]).wait()

    def scores(keys, j, held_scores):
        s = lax.dot_general(
            keys, qbuf[j], (((1,), (1,)), ((), ())), preferred_element_type=jnp.float32
        )
        held_scores[...] = s
        old = mx[j, 0:1, :]
        new = jnp.maximum(old, jnp.max(s, axis=0, keepdims=True))
        mx[j, 0:1, :] = new
        return old, new

    def update(j, s, old, new, vt_rows):
        p = jnp.exp2((s - new) * EXP2_SCALE).astype(jnp.bfloat16)
        fade = jnp.exp2((old - new) * EXP2_SCALE)
        part = jnp.dot(vt_rows, p, preferred_element_type=jnp.float32)
        acc[j] = acc[j] * fade + part

    def sweep(first, count, ready=None, done=None):
        rows = pl.ds(first, count)
        buffers = (sa.at[pl.ds(0, count)], sb.at[pl.ds(0, count)])

        def begin(k):
            if ready is not None:
                ready(k)
            return scores(kp[rows, :], chunks[k], buffers[k % 2])

        state = begin(0)
        for k in range(N_HOME):
            ahead = begin(k + 1) if k + 1 < N_HOME else None
            update(chunks[k], buffers[k % 2][...], *state, vt[:, rows])
            if done is not None:
                done(chunks[k])
            state = ahead

    position = lax.broadcasted_iota(jnp.int32, (HALF, HD), 0)
    lane_position = lax.broadcasted_iota(jnp.int32, (16, HD), 1)
    first_row = lax.broadcasted_iota(jnp.int32, (16, HD), 0) == 0

    def arrive(b, at_key):
        oi = b // 2
        cross = b % 2
        for h in range(2):
            rows = pl.ds(h * HALF, HALF)
            slot = cross * (1 + h)
            if b > 0 and (cross or h == 0):
                pltpu.make_async_copy(lst.at[0, 0], lbuf.at[oi, slot], l_recv.at[oi, slot]).wait()
            pltpu.make_async_copy(ck_ref.at[0, rows], kbuf.at[b, rows], kv_recv.at[b, h, 0]).wait()
            pltpu.make_async_copy(cv_ref.at[0, rows], vbuf.at[b, rows], kv_recv.at[b, h, 1]).wait()
        spare = kbuf[0, 0:16, :].astype(jnp.float32)[0:1, :]
        for h in range(2):
            rows = pl.ds(h * HALF, HALF)
            put = pl.ds(at_key + h * HALF, HALF)
            fill = lbuf[oi, cross * (1 + h)]
            ok = position + h * HALF < fill[0:1, :]
            keys = kbuf[b, rows, :].astype(jnp.float32)
            kp[put, :] = jnp.where(ok, keys, spare).astype(jnp.bfloat16)
            values = jnp.where(ok, vbuf[b, rows, :].astype(jnp.float32), 0.0)
            vt[0:HD, put] = values.T.astype(jnp.bfloat16)
            for g in range(HALF // HD):
                first = h * HALF + g * HD
                counted = first_row & (lane_position + first < fill[0:1, :])
                vt[HD:VROWS, pl.ds(at_key + first, HD)] = jnp.where(counted, 1.0, 0.0).astype(
                    jnp.bfloat16
                )

    for first, second in ((0, 1), (2, 4), (3, 5)):
        arrive(first, 0)
        arrive(second, SHARD)
        sweep(0, 2 * SHARD, ready=queries_here if first == 0 else None)

    for kv in range(2):
        pltpu.make_async_copy(
            (nk_ref, nv_ref)[kv], (nkbuf, nvbuf)[kv], n_recv.at[kv]
        ).wait()
    vtn[0:HD, :] = nvbuf[...].astype(jnp.float32).T.astype(jnp.bfloat16)
    ones = lax.broadcasted_iota(jnp.int32, (16, HOME_ROWS), 0) == 0
    vtn[HD:VROWS, :] = jnp.where(ones, 1.0, 0.0).astype(jnp.bfloat16)
    key_pos = (z // 2) * HOME_ROWS + lax.broadcasted_iota(jnp.int32, (HOME_ROWS, QC), 0)
    row_pos = lax.broadcasted_iota(jnp.int32, (HOME_ROWS, QC), 1) % HOME_ROWS
    begun = key_pos >= start_ref[held]
    for j in range(N_HOME):
        s = lax.dot_general(
            nkbuf[...], qbuf[j], (((1,), (1,)), ((), ())), preferred_element_type=jnp.float32
        )
        s = jnp.where(begun & (key_pos <= row_pos + j * HOME_ROWS), s, MASKED)
        old = mx[j, 0:1, :]
        new = jnp.maximum(old, jnp.max(s, axis=0, keepdims=True))
        mx[j, 0:1, :] = new
        update(j, s, old, new, vtn[...])

    arrive(2 * NY - 1, 0)
    sweep(0, SHARD)
    arrive(2 * NY - 2, 0)

    def o_pairs(j, g):
        me = z // 2
        return (
            (ost.at[j, g], obuf.at[me, g], o_send.at[j, g], o_recv.at[me, g]),
            (sst.at[j, g], sbuf.at[me, g], s_send.at[j, g], s_recv.at[me, g]),
        )

    def send_partial(j, g):
        for i in range(GL // 128):
            lanes = pl.ds(g * GL + i * 128, 128)
            sst[j, g, i : i + 1, :] = mx[j, 0:1, lanes]
            sst[j, g, 4 + i : 5 + i, :] = acc[j, HD : HD + 1, lanes]
        ost[j, g] = acc[j, 0:HD, pl.ds(g * GL, GL)].astype(jnp.bfloat16)

        @pl.when(4 * par + j != z)
        def _():
            for src, dst, send, recv in o_pairs(j, g):
                remote(src, dst, send, recv, at(y, 4 * par + j)).start()

        @pl.when(4 * par + j == z)
        def _():
            for src, dst, send, recv in o_pairs(j, g):
                pltpu.make_async_copy(src, dst, recv).start()

    sweep(0, SHARD, done=lambda j: send_partial(j, 0))
    for j in chunks:
        send_partial(j, 1)

    w_copy.wait()

    def attend_group(g):
        for i in range(N_HOME):
            pltpu.make_async_copy(ost.at[0, g], obuf.at[i, g], o_recv.at[i, g]).wait()
            pltpu.make_async_copy(sst.at[0, g], sbuf.at[i, g], s_recv.at[i, g]).wait()

        def stat(i, first):
            rows = [sbuf[i, g, first + n : first + n + 1, :] for n in range(GL // 128)]
            return jnp.concatenate(rows, axis=1)

        highest = [stat(i, 0) for i in range(N_HOME)]
        top = highest[0]
        for i in range(1, N_HOME):
            top = jnp.maximum(top, highest[i])
        total = jnp.zeros((1, GL), jnp.float32)
        summed = jnp.zeros((HD, GL), jnp.float32)
        for i in range(N_HOME):
            factor = jnp.exp2((highest[i] - top) * EXP2_SCALE)
            total = total + factor * stat(i, 4)
            summed = summed + factor * obuf[i, g].astype(jnp.float32)
        attended = (summed / total).T
        for n in range(GL // HOME_ROWS):
            att[g, :, pl.ds(n * HD, HD)] = attended[n * HOME_ROWS : (n + 1) * HOME_ROWS].astype(
                jnp.bfloat16
            )

    depth = GROUP * HD // 2
    attend_group(0)
    for c in range(2 * N_COL):
        cols = pl.ds(c * (COL // 2), COL // 2)
        proj[:, cols] = jnp.dot(
            att[0], wbuf[pl.ds(0, depth), cols], preferred_element_type=jnp.float32
        )
    attend_group(1)

    def c_copy(c):
        return remote(
            pst.at[c, 1 - core], cbuf.at[c], c_send.at[c], c_recv.at[c], sibling
        )

    def p_copy(c, d):
        to = (x + d) % NX
        return remote(
            xst.at[c, to], rbuf.at[c, x], p_send.at[c, d], p_recv.at[c, x], across(d)
        )

    def project(c):
        for g in range(2):
            cols = pl.ds(c * COL + g * (COL // 2), COL // 2)
            prod = proj[:, cols] + jnp.dot(
                att[1], wbuf[pl.ds(depth, depth), cols], preferred_element_type=jnp.float32
            )
            for t in range(NTP):
                pst[c, t % 2, t // 2, pl.ds(g * 8, 8), :] = prod[t * 8 : (t + 1) * 8, :].astype(
                    jnp.bfloat16
                )
        c_copy(c).start()

    def to_owners(c):
        pltpu.make_async_copy(pst.at[c, 0], cbuf.at[c], c_recv.at[c]).wait()
        xst[c] = (pst[c, core].astype(jnp.float32) + cbuf[c].astype(jnp.float32)).astype(jnp.bfloat16)
        for d in range(1, NX):
            p_copy(c, d).start()

    project(0)
    for c in range(1, N_COL):
        project(c)
        to_owners(c - 1)
    to_owners(N_COL - 1)

    for c in range(N_COL):
        sums = xst[c, x].astype(jnp.float32)
        for d in range(1, NX):
            source = (x + d) % NX
            pltpu.make_async_copy(xst.at[c, 0], rbuf.at[c, source], p_recv.at[c, source]).wait()
            sums = sums + rbuf[c, source].astype(jnp.float32)
        for g in range(2):
            out_ref[:, pl.ds(c * COL + g * (COL // 2), COL // 2)] = sums[g * 8 : (g + 1) * 8].astype(
                jnp.bfloat16
            )

    for i in range(N_HOME):

        @pl.when(2 * i + home_par != z)
        def _():
            q_copy(i).wait_send()

    for kv in range(2):

        @pl.when(new_target != z)
        def _():
            n_copy(kv).wait_send()

    for copy in l_copies + [copy for block in by_block.values() for copy in block]:
        copy.wait_send()
    for j in range(N_HOME):

        @pl.when(4 * par + j != z)
        def _():
            for g in range(2):
                for src, dst, send, recv in o_pairs(j, g):
                    remote(src, dst, send, recv, at(y, 4 * par + j)).wait_send()

    for c in range(N_COL):
        c_copy(c).wait_send()
        for d in range(1, NX):
            p_copy(c, d).wait_send()


def on_device(queries, new_keys, new_values, cache_keys, cache_values, lengths, turn_start, out_weight):
    vmem = pl.BlockSpec(memory_space=pltpu.VMEM)
    hbm = pl.BlockSpec(memory_space=pl.ANY)
    bf16, f32, i32 = jnp.bfloat16, jnp.float32, jnp.int32
    dma = pltpu.SemaphoreType.DMA
    return pl.pallas_call(
        kernel,
        out_shape=jax.ShapeDtypeStruct((HOME_ROWS // NTP, OUT), bf16),
        in_specs=[hbm] * 8,
        out_specs=vmem,
        scratch_shapes=[
            pltpu.VMEM((HOME_ROWS, GROUP * HD), bf16),
            pltpu.SMEM((1, 8), i32),
            pltpu.SMEM((8,), i32),
            pltpu.VMEM((QC, HD), bf16),
            pltpu.VMEM((N_HOME, QC, HD), bf16),
            pltpu.VMEM((2 * NY, SHARD, HD), bf16),
            pltpu.VMEM((2 * NY, SHARD, HD), bf16),
            pltpu.VMEM((2 * SHARD, HD), bf16),
            pltpu.VMEM((VROWS, 2 * SHARD), bf16),
            pltpu.VMEM((2 * SHARD, QC), f32),
            pltpu.VMEM((2 * SHARD, QC), f32),
            pltpu.VMEM((NY, 2, 8, 128), i32),
            pltpu.VMEM((NY, 3, 8, 128), i32),
            pltpu.VMEM((HOME_ROWS, HD), bf16),
            pltpu.VMEM((HOME_ROWS, HD), bf16),
            pltpu.VMEM((VROWS, HOME_ROWS), bf16),
            pltpu.VMEM((N_HOME, VROWS, QC), f32),
            pltpu.VMEM((N_HOME, 8, QC), f32),
            pltpu.VMEM((N_HOME, 2, HD, GL), bf16),
            pltpu.VMEM((N_HOME, 2, 8, 128), f32),
            pltpu.VMEM((N_HOME, 2, HD, GL), bf16),
            pltpu.VMEM((N_HOME, 2, 8, 128), f32),
            pltpu.VMEM((2, HOME_ROWS, GROUP * HD // 2), bf16),
            pltpu.VMEM((HOME_ROWS, OUT), f32),
            pltpu.VMEM((GROUP * HD, OUT), bf16),
            pltpu.VMEM((N_COL, 2, NX, 16, COL // 2), bf16),
            pltpu.VMEM((N_COL, NX, 16, COL // 2), bf16),
            pltpu.VMEM((N_COL, NX, 16, COL // 2), bf16),
            pltpu.VMEM((N_COL, NX, 16, COL // 2), bf16),
            dma((3,)),
            dma,
            dma((2 * NY, 2, 2)),
            dma((2 * NY, 2, 2)),
            dma((NY, 3)),
            dma((NY, 3)),
            dma((N_HOME,)),
            dma((N_HOME,)),
            dma((2,)),
            dma((2,)),
            dma((N_HOME, 2)),
            dma((N_HOME, 2)),
            dma((N_HOME, 2)),
            dma((N_HOME, 2)),
            dma((N_COL,)),
            dma((N_COL,)),
            dma((N_COL, NX)),
            dma((N_COL, NX)),
        ],
        compiler_params=pltpu.CompilerParams(
            collective_id=0, has_side_effects=True, vmem_limit_bytes=60 << 20
        ),
        name="attend_project",
    )(queries, new_keys, new_values, cache_keys, cache_values, lengths.T, turn_start, out_weight)


def solution(mesh):
    in_specs = (
        P("ctx", "tp"),
        P("ctx", "tp"),
        P("ctx", "tp"),
        P(None, "ctx", "tp"),
        P(None, "ctx", "tp"),
        P(None, "ctx"),
        P(),
        P("tp", None),
    )
    return jax.shard_map(
        on_device, mesh=mesh, in_specs=in_specs, out_specs=P(("ctx", "tp"), None), check_vma=False
    )
```

```python
import math

import jax
import jax.numpy as jnp
from jax import lax
from jax.experimental import pallas as pl
from jax.experimental.pallas import tpu as pltpu
from jax.sharding import PartitionSpec as P

HD = 128
GROUP = 8
NY = 4
NZ = 8
NTP = 8
NX = 4
SHARD = 768
HALF = SHARD // 2
HOME_ROWS = 64
QC = GROUP * HOME_ROWS
N_HOME = 4
GL = QC // 2
OUT = 4096
VROWS = HD + 16
MASKED = -1e30
EXP2_SCALE = math.log2(math.e) / math.sqrt(HD)
DY = (0, 1, 3, 2)
N_COL = 4
COL = OUT // N_COL
MESH = pl.DeviceIdType.MESH
ORDER = (2, 4, -1, -2, -3, -4, 1, 3, 5, 6, 7)


def kernel(
    q_hbm, nk_ref, nv_ref, ck_ref, cv_ref, len_hbm, start_hbm, w_ref, out_ref,
    q_ref, len_ref, start_ref, qst, qbuf, kbuf, vbuf, kp, vt, sa, sb, lst, lbuf, nkbuf, nvbuf, vtn, acc, mx,
    ost, sst, obuf, sbuf, att, proj, wbuf, pst, cbuf, xst, rbuf,
    in_sem, w_sem, kv_send, kv_recv, l_send, l_recv, q_send, q_recv,
    n_send, n_recv, o_send, o_recv, s_send, s_recv, c_send, c_recv, p_send, p_recv,
):
    ctx = lax.axis_index("ctx")
    tp = lax.axis_index("tp")
    y = ctx // NZ
    z = ctx % NZ
    x = tp // 2
    core = tp % 2
    par = z % 2
    held = 2 * y + par
    home_par = z // 4
    home_slot = z % 4

    def at(row, col):
        return {"ctx": row * NZ + col, "tp": tp}

    sibling = {"ctx": ctx, "tp": tp // 2 * 2 + 1 - core}

    def across(d):
        return {"ctx": ctx, "tp": (x + d) % NX * 2 + core}

    def row_of(oi):
        return (y + DY[oi]) % NY

    inputs = [
        pltpu.make_async_copy(src, dst, in_sem.at[i])
        for i, (src, dst) in enumerate(((q_hbm, q_ref), (len_hbm, len_ref), (start_hbm, start_ref)))
    ]
    for copy in inputs:
        copy.start()

    barrier = pltpu.get_barrier_semaphore()
    n_peers = 0
    for dy in range(NY):
        for dz in range(NZ):
            if (dy == 0 and dz != 0) or (dy != 0 and dz in (0, 1, NZ - 1)):
                pl.semaphore_signal(
                    barrier, inc=1, device_id=at((y + dy) % NY, (z + dz) % NZ), device_id_type=MESH
                )
                n_peers += 1
    for peer in [sibling] + [across(d) for d in range(1, NX)]:
        pl.semaphore_signal(barrier, inc=1, device_id=peer, device_id_type=MESH)
        n_peers += 1

    w_copy = pltpu.make_async_copy(w_ref, wbuf, w_sem)
    own = []
    for h in range(2):
        rows = pl.ds(h * HALF, HALF)
        for kv, (src, dst) in enumerate(((ck_ref, kbuf), (cv_ref, vbuf))):
            own.append(
                pltpu.make_async_copy(
                    src.at[held, rows], dst.at[0, rows], kv_recv.at[0, h, kv]
                )
            )
    for copy in own:
        copy.start()
    w_copy.start()
    for copy in inputs:
        copy.wait()
    for g in range(GROUP):
        qst[pl.ds(g * HOME_ROWS, HOME_ROWS), :] = q_ref[:, pl.ds(g * HD, HD)]
    for oi in range(NY):
        row = row_of(oi)
        lst[oi, 0] = jnp.full((8, 128), len_ref[0, 2 * row + par], jnp.int32)
        lst[oi, 1] = jnp.full((8, 128), len_ref[0, 2 * row + 1 - par], jnp.int32)
    lbuf[0, 0] = lst[0, 0]

    pl.semaphore_wait(barrier, n_peers)

    def remote(src, dst, send, recv, device):
        return pltpu.make_async_remote_copy(
            src_ref=src, dst_ref=dst, send_sem=send, recv_sem=recv,
            device_id=device, device_id_type=MESH,
        )

    by_block = {}
    l_copies = []
    for oi in range(NY):
        row = row_of(oi)
        for cross in range(2):
            if oi == 0 and cross == 0:
                continue
            traj = 2 * row + (1 - par if cross else par)
            for h in range(2):
                dz = 0 if not cross else (1 if h == 0 else NZ - 1)
                device = at(row, (z + dz) % NZ)
                if cross or h == 0:
                    slot = 0 if not cross else 1 + h
                    l_copies.append(
                        remote(
                            lst.at[oi, cross], lbuf.at[oi, slot],
                            l_send.at[oi, slot], l_recv.at[oi, slot], device,
                        )
                    )
                rows = pl.ds(h * HALF, HALF)
                for kv, (src, dst) in enumerate(((ck_ref, kbuf), (cv_ref, vbuf))):
                    b = 2 * oi + cross
                    copy = remote(
                        src.at[traj, rows], dst.at[b, rows],
                        kv_send.at[b, h, kv], kv_recv.at[b, h, kv], device,
                    )
                    by_block.setdefault(2 * oi + cross, []).append(copy)
    def q_copy(i):
        return remote(
            qst, qbuf.at[home_slot], q_send.at[i], q_recv.at[home_slot], at(y, 2 * i + home_par)
        )

    def q_local():
        return pltpu.make_async_copy(qst, qbuf.at[home_slot], q_recv.at[home_slot])

    def send_queries(i):
        target = 2 * i + home_par

        @pl.when(target != z)
        def _():
            q_copy(i).start()

        @pl.when(target == z)
        def _():
            q_local().start()

    new_target = 2 * home_slot + home_par

    def n_copy(kv):
        return remote(
            (nk_ref, nv_ref)[kv], (nkbuf, nvbuf)[kv], n_send.at[kv], n_recv.at[kv], at(y, new_target)
        )

    def n_local(kv):
        return pltpu.make_async_copy((nk_ref, nv_ref)[kv], (nkbuf, nvbuf)[kv], n_recv.at[kv])

    for kv in range(2):

        @pl.when(new_target != z)
        def _():
            n_copy(kv).start()

        @pl.when(new_target == z)
        def _():
            n_local(kv).start()

    for copy in l_copies:
        copy.start()

    for item in ORDER:
        if item < 0:
            send_queries(-1 - item)
        else:
            for copy in by_block[item]:
                copy.start()

    acc[...] = jnp.zeros_like(acc)
    mx[...] = jnp.full_like(mx, MASKED)
    sst[...] = jnp.zeros_like(sst)

    chunks = list(range(N_HOME))

    def queries_here(k):
        pltpu.make_async_copy(qst, qbuf.at[chunks[k]], q_recv.at[chunks[k]]).wait()

    def scores(keys, j, held_scores):
        s = lax.dot_general(
            keys, qbuf[j], (((1,), (1,)), ((), ())), preferred_element_type=jnp.float32
        )
        held_scores[...] = s
        old = mx[j, 0:1, :]
        new = jnp.maximum(old, jnp.max(s, axis=0, keepdims=True))
        mx[j, 0:1, :] = new
        return old, new

    def update(j, s, old, new, vt_rows):
        p = jnp.exp2((s - new) * EXP2_SCALE).astype(jnp.bfloat16)
        fade = jnp.exp2((old - new) * EXP2_SCALE)
        part = jnp.dot(vt_rows, p, preferred_element_type=jnp.float32)
        acc[j] = acc[j] * fade + part

    def sweep(first, count, ready=None, done=None):
        rows = pl.ds(first, count)
        buffers = (sa.at[pl.ds(0, count)], sb.at[pl.ds(0, count)])

        def begin(k):
            if ready is not None:
                ready(k)
            return scores(kp[rows, :], chunks[k], buffers[k % 2])

        state = begin(0)
        for k in range(N_HOME):
            ahead = begin(k + 1) if k + 1 < N_HOME else None
            update(chunks[k], buffers[k % 2][...], *state, vt[:, rows])
            if done is not None:
                done(chunks[k])
            state = ahead

    position = lax.broadcasted_iota(jnp.int32, (HALF, HD), 0)
    lane_position = lax.broadcasted_iota(jnp.int32, (16, HD), 1)
    first_row = lax.broadcasted_iota(jnp.int32, (16, HD), 0) == 0

    def arrive(b, at_key):
        oi = b // 2
        cross = b % 2
        for h in range(2):
            rows = pl.ds(h * HALF, HALF)
            slot = cross * (1 + h)
            if b > 0 and (cross or h == 0):
                pltpu.make_async_copy(lst.at[0, 0], lbuf.at[oi, slot], l_recv.at[oi, slot]).wait()
            pltpu.make_async_copy(ck_ref.at[0, rows], kbuf.at[b, rows], kv_recv.at[b, h, 0]).wait()
            pltpu.make_async_copy(cv_ref.at[0, rows], vbuf.at[b, rows], kv_recv.at[b, h, 1]).wait()
        spare = kbuf[0, 0:16, :].astype(jnp.float32)[0:1, :]
        for h in range(2):
            rows = pl.ds(h * HALF, HALF)
            put = pl.ds(at_key + h * HALF, HALF)
            fill = lbuf[oi, cross * (1 + h)]
            ok = position + h * HALF < fill[0:1, :]
            keys = kbuf[b, rows, :].astype(jnp.float32)
            kp[put, :] = jnp.where(ok, keys, spare).astype(jnp.bfloat16)
            values = jnp.where(ok, vbuf[b, rows, :].astype(jnp.float32), 0.0)
            vt[0:HD, put] = values.T.astype(jnp.bfloat16)
            for g in range(HALF // HD):
                first = h * HALF + g * HD
                counted = first_row & (lane_position + first < fill[0:1, :])
                vt[HD:VROWS, pl.ds(at_key + first, HD)] = jnp.where(counted, 1.0, 0.0).astype(
                    jnp.bfloat16
                )

    for oi in range(NY - 1):
        arrive(2 * oi, 0)
        arrive(2 * oi + 1, SHARD)
        sweep(0, 2 * SHARD, ready=queries_here if oi == 0 else None)

    for kv in range(2):
        pltpu.make_async_copy(
            (nk_ref, nv_ref)[kv], (nkbuf, nvbuf)[kv], n_recv.at[kv]
        ).wait()
    vtn[0:HD, :] = nvbuf[...].astype(jnp.float32).T.astype(jnp.bfloat16)
    ones = lax.broadcasted_iota(jnp.int32, (16, HOME_ROWS), 0) == 0
    vtn[HD:VROWS, :] = jnp.where(ones, 1.0, 0.0).astype(jnp.bfloat16)
    key_pos = (z // 2) * HOME_ROWS + lax.broadcasted_iota(jnp.int32, (HOME_ROWS, QC), 0)
    row_pos = lax.broadcasted_iota(jnp.int32, (HOME_ROWS, QC), 1) % HOME_ROWS
    begun = key_pos >= start_ref[held]
    for j in range(N_HOME):
        s = lax.dot_general(
            nkbuf[...], qbuf[j], (((1,), (1,)), ((), ())), preferred_element_type=jnp.float32
        )
        s = jnp.where(begun & (key_pos <= row_pos + j * HOME_ROWS), s, MASKED)
        old = mx[j, 0:1, :]
        new = jnp.maximum(old, jnp.max(s, axis=0, keepdims=True))
        mx[j, 0:1, :] = new
        update(j, s, old, new, vtn[...])

    arrive(2 * NY - 2, 0)
    sweep(0, SHARD)
    arrive(2 * NY - 1, 0)

    def o_pairs(j, g):
        me = z // 2
        return (
            (ost.at[j, g], obuf.at[me, g], o_send.at[j, g], o_recv.at[me, g]),
            (sst.at[j, g], sbuf.at[me, g], s_send.at[j, g], s_recv.at[me, g]),
        )

    def send_partial(j, g):
        for i in range(GL // 128):
            lanes = pl.ds(g * GL + i * 128, 128)
            sst[j, g, i : i + 1, :] = mx[j, 0:1, lanes]
            sst[j, g, 4 + i : 5 + i, :] = acc[j, HD : HD + 1, lanes]
        ost[j, g] = acc[j, 0:HD, pl.ds(g * GL, GL)].astype(jnp.bfloat16)

        @pl.when(4 * par + j != z)
        def _():
            for src, dst, send, recv in o_pairs(j, g):
                remote(src, dst, send, recv, at(y, 4 * par + j)).start()

        @pl.when(4 * par + j == z)
        def _():
            for src, dst, send, recv in o_pairs(j, g):
                pltpu.make_async_copy(src, dst, recv).start()

    sweep(0, SHARD, done=lambda j: send_partial(j, 0))
    for j in chunks:
        send_partial(j, 1)

    w_copy.wait()

    def attend_group(g):
        for i in range(N_HOME):
            pltpu.make_async_copy(ost.at[0, g], obuf.at[i, g], o_recv.at[i, g]).wait()
            pltpu.make_async_copy(sst.at[0, g], sbuf.at[i, g], s_recv.at[i, g]).wait()

        def stat(i, first):
            rows = [sbuf[i, g, first + n : first + n + 1, :] for n in range(GL // 128)]
            return jnp.concatenate(rows, axis=1)

        highest = [stat(i, 0) for i in range(N_HOME)]
        top = highest[0]
        for i in range(1, N_HOME):
            top = jnp.maximum(top, highest[i])
        total = jnp.zeros((1, GL), jnp.float32)
        summed = jnp.zeros((HD, GL), jnp.float32)
        for i in range(N_HOME):
            factor = jnp.exp2((highest[i] - top) * EXP2_SCALE)
            total = total + factor * stat(i, 4)
            summed = summed + factor * obuf[i, g].astype(jnp.float32)
        attended = (summed / total).T
        for n in range(GL // HOME_ROWS):
            att[g, :, pl.ds(n * HD, HD)] = attended[n * HOME_ROWS : (n + 1) * HOME_ROWS].astype(
                jnp.bfloat16
            )

    depth = GROUP * HD // 2
    attend_group(0)
    for c in range(2 * N_COL):
        cols = pl.ds(c * (COL // 2), COL // 2)
        proj[:, cols] = jnp.dot(
            att[0], wbuf[pl.ds(0, depth), cols], preferred_element_type=jnp.float32
        )
    attend_group(1)

    def c_copy(c):
        return remote(
            pst.at[c, 1 - core], cbuf.at[c], c_send.at[c], c_recv.at[c], sibling
        )

    def p_copy(c, d):
        to = (x + d) % NX
        return remote(
            xst.at[c, to], rbuf.at[c, x], p_send.at[c, d], p_recv.at[c, x], across(d)
        )

    def project(c):
        for g in range(2):
            cols = pl.ds(c * COL + g * (COL // 2), COL // 2)
            prod = proj[:, cols] + jnp.dot(
                att[1], wbuf[pl.ds(depth, depth), cols], preferred_element_type=jnp.float32
            )
            for t in range(NTP):
                pst[c, t % 2, t // 2, pl.ds(g * 8, 8), :] = prod[t * 8 : (t + 1) * 8, :].astype(
                    jnp.bfloat16
                )
        c_copy(c).start()

    def to_owners(c):
        pltpu.make_async_copy(pst.at[c, 0], cbuf.at[c], c_recv.at[c]).wait()
        xst[c] = (pst[c, core].astype(jnp.float32) + cbuf[c].astype(jnp.float32)).astype(jnp.bfloat16)
        for d in range(1, NX):
            p_copy(c, d).start()

    project(0)
    for c in range(1, N_COL):
        project(c)
        to_owners(c - 1)
    to_owners(N_COL - 1)

    for c in range(N_COL):
        sums = xst[c, x].astype(jnp.float32)
        for d in range(1, NX):
            source = (x + d) % NX
            pltpu.make_async_copy(xst.at[c, 0], rbuf.at[c, source], p_recv.at[c, source]).wait()
            sums = sums + rbuf[c, source].astype(jnp.float32)
        for g in range(2):
            out_ref[:, pl.ds(c * COL + g * (COL // 2), COL // 2)] = sums[g * 8 : (g + 1) * 8].astype(
                jnp.bfloat16
            )

    for i in range(N_HOME):

        @pl.when(2 * i + home_par != z)
        def _():
            q_copy(i).wait_send()

    for kv in range(2):

        @pl.when(new_target != z)
        def _():
            n_copy(kv).wait_send()

    for copy in l_copies + [copy for block in by_block.values() for copy in block]:
        copy.wait_send()
    for j in range(N_HOME):

        @pl.when(4 * par + j != z)
        def _():
            for g in range(2):
                for src, dst, send, recv in o_pairs(j, g):
                    remote(src, dst, send, recv, at(y, 4 * par + j)).wait_send()

    for c in range(N_COL):
        c_copy(c).wait_send()
        for d in range(1, NX):
            p_copy(c, d).wait_send()


def on_device(queries, new_keys, new_values, cache_keys, cache_values, lengths, turn_start, out_weight):
    vmem = pl.BlockSpec(memory_space=pltpu.VMEM)
    hbm = pl.BlockSpec(memory_space=pl.ANY)
    bf16, f32, i32 = jnp.bfloat16, jnp.float32, jnp.int32
    dma = pltpu.SemaphoreType.DMA
    return pl.pallas_call(
        kernel,
        out_shape=jax.ShapeDtypeStruct((HOME_ROWS // NTP, OUT), bf16),
        in_specs=[hbm] * 8,
        out_specs=vmem,
        scratch_shapes=[
            pltpu.VMEM((HOME_ROWS, GROUP * HD), bf16),
            pltpu.SMEM((1, 8), i32),
            pltpu.SMEM((8,), i32),
            pltpu.VMEM((QC, HD), bf16),
            pltpu.VMEM((N_HOME, QC, HD), bf16),
            pltpu.VMEM((2 * NY, SHARD, HD), bf16),
            pltpu.VMEM((2 * NY, SHARD, HD), bf16),
            pltpu.VMEM((2 * SHARD, HD), bf16),
            pltpu.VMEM((VROWS, 2 * SHARD), bf16),
            pltpu.VMEM((2 * SHARD, QC), f32),
            pltpu.VMEM((2 * SHARD, QC), f32),
            pltpu.VMEM((NY, 2, 8, 128), i32),
            pltpu.VMEM((NY, 3, 8, 128), i32),
            pltpu.VMEM((HOME_ROWS, HD), bf16),
            pltpu.VMEM((HOME_ROWS, HD), bf16),
            pltpu.VMEM((VROWS, HOME_ROWS), bf16),
            pltpu.VMEM((N_HOME, VROWS, QC), f32),
            pltpu.VMEM((N_HOME, 8, QC), f32),
            pltpu.VMEM((N_HOME, 2, HD, GL), bf16),
            pltpu.VMEM((N_HOME, 2, 8, 128), f32),
            pltpu.VMEM((N_HOME, 2, HD, GL), bf16),
            pltpu.VMEM((N_HOME, 2, 8, 128), f32),
            pltpu.VMEM((2, HOME_ROWS, GROUP * HD // 2), bf16),
            pltpu.VMEM((HOME_ROWS, OUT), f32),
            pltpu.VMEM((GROUP * HD, OUT), bf16),
            pltpu.VMEM((N_COL, 2, NX, 16, COL // 2), bf16),
            pltpu.VMEM((N_COL, NX, 16, COL // 2), bf16),
            pltpu.VMEM((N_COL, NX, 16, COL // 2), bf16),
            pltpu.VMEM((N_COL, NX, 16, COL // 2), bf16),
            dma((3,)),
            dma,
            dma((2 * NY, 2, 2)),
            dma((2 * NY, 2, 2)),
            dma((NY, 3)),
            dma((NY, 3)),
            dma((N_HOME,)),
            dma((N_HOME,)),
            dma((2,)),
            dma((2,)),
            dma((N_HOME, 2)),
            dma((N_HOME, 2)),
            dma((N_HOME, 2)),
            dma((N_HOME, 2)),
            dma((N_COL,)),
            dma((N_COL,)),
            dma((N_COL, NX)),
            dma((N_COL, NX)),
        ],
        compiler_params=pltpu.CompilerParams(
            collective_id=0, has_side_effects=True, vmem_limit_bytes=60 << 20
        ),
        name="attend_project",
    )(queries, new_keys, new_values, cache_keys, cache_values, lengths.T, turn_start, out_weight)


def solution(mesh):
    in_specs = (
        P("ctx", "tp"),
        P("ctx", "tp"),
        P("ctx", "tp"),
        P(None, "ctx", "tp"),
        P(None, "ctx", "tp"),
        P(None, "ctx"),
        P(),
        P("tp", None),
    )
    return jax.shard_map(
        on_device, mesh=mesh, in_specs=in_specs, out_specs=P(("ctx", "tp"), None), check_vma=False
    )
```
